32 devices in a mesh: dp: 8 (over z, y), ctx: 4 (over x, core).
Axes of the slice: x: 2, y: 2, z: 4, core: 2. Of those that a mesh axis runs over, the one named last changes fastest.
Arguments:
- tokens: bfloat16 [16, 1024, 1024], P('dp', 'ctx'), may hold values from -6 to 6
- segments: int32 [16, 1024], P('dp', 'ctx'), may hold values from 0 to 2, as said below
- pre_gain: bfloat16 [1024], P(('dp', 'ctx')), may hold values from 0.5 to 1.5
- gate_proj: bfloat16 [1024, 1536], P(('dp', 'ctx')), may hold values from -0.1875 to 0.1875
- mix_proj: bfloat16 [1024, 1792], P(('dp', 'ctx')), may hold values from -0.1875 to 0.1875
- step_proj: bfloat16 [1024, 24], P(('dp', 'ctx')), may hold values from -0.1875 to 0.1875
- conv_taps: bfloat16 [4, 1792], P(None, ('dp', 'ctx')), may hold values from -3 to 3
- conv_bias: bfloat16 [1792], P(('dp', 'ctx')), may hold values from -2 to 2
- decay_log: float32 [24], replicated, may hold values from -7.5 to -2.5
- step_bias: float32 [24], replicated, may hold values from -3 to -0.5
- skip_scale: float32 [24], replicated, may hold values from 0.5 to 1.5
- inner_gain: bfloat16 [1536], P(('dp', 'ctx')), may hold values from 0.5 to 1.5
- mamba_proj: bfloat16 [1536, 1024], P(('dp', 'ctx')), may hold values from -0.15625 to 0.15625
- query_proj: bfloat16 [1024, 1024], P(('dp', 'ctx')), may hold values from -0.1875 to 0.1875
- key_proj: bfloat16 [1024, 256], P(('dp', 'ctx')), may hold values from -0.1875 to 0.1875
- value_proj: bfloat16 [1024, 256], P(('dp', 'ctx')), may hold values from -0.1875 to 0.1875
- attn_proj: bfloat16 [1024, 1024], P(('dp', 'ctx')), may hold values from -0.75 to 0.75
- feed_gain: bfloat16 [1024], P(('dp', 'ctx')), may hold values from 0.5 to 1.5
- feed_gate: bfloat16 [1024, 2048], P(('dp', 'ctx')), may hold values from -0.1875 to 0.1875
- feed_up: bfloat16 [1024, 2048], P(('dp', 'ctx')), may hold values from -0.1875 to 0.1875
- feed_down: bfloat16 [2048, 1024], P(('dp', 'ctx')), may hold values from -0.125 to 0.125
- cotangent: bfloat16 [16, 1024, 1024], P('dp', 'ctx'), may hold values from -6 to 6
Outputs:
- output: bfloat16 [16, 1024, 1024], P('dp', 'ctx')
- grad_tokens: float32 [16, 1024, 1024], P('dp', 'ctx')
- grad_pre_gain: float32 [1024], P(('dp', 'ctx'))
- grad_gate_proj: float32 [1024, 1536], P(('dp', 'ctx'))
- grad_mix_proj: float32 [1024, 1792], P(('dp', 'ctx'))
- grad_step_proj: float32 [1024, 24], P(('dp', 'ctx'))
- grad_conv_taps: float32 [4, 1792], P(None, ('dp', 'ctx'))
- grad_conv_bias: float32 [1792], P(('dp', 'ctx'))
- grad_decay_log: float32 [24], replicated
- grad_step_bias: float32 [24], replicated
- grad_skip_scale: float32 [24], replicated
- grad_inner_gain: float32 [1536], P(('dp', 'ctx'))
- grad_mamba_proj: float32 [1536, 1024], P(('dp', 'ctx'))
- grad_query_proj: float32 [1024, 1024], P(('dp', 'ctx'))
- grad_key_proj: float32 [1024, 256], P(('dp', 'ctx'))
- grad_value_proj: float32 [1024, 256], P(('dp', 'ctx'))
- grad_attn_proj: float32 [1024, 1024], P(('dp', 'ctx'))
- grad_feed_gain: float32 [1024], P(('dp', 'ctx'))
- grad_feed_gate: float32 [1024, 2048], P(('dp', 'ctx'))
- grad_feed_up: float32 [1024, 2048], P(('dp', 'ctx'))
- grad_feed_down: float32 [2048, 1024], P(('dp', 'ctx'))
The draws below stay inside these ranges and needn't reach their ends.
Inputs may be any that keep to these rules, and one draw needn't show every extreme that they name: `segments`: each sequence's segment numbers start at 0 and rise by one at each new document; every document has at least 1024 // 3 - 2 * (64) tokens. In each group of 2 sequences on one index of dp, one sequence is a single document and another holds three.
All inputs are finite; a program needn't handle non-finite values.
Results may differ from the reference program's by a relative error of at most 0.015.
Values may be sent and summed in bfloat16 or wider, within the bound.
A program may use at most 256 MiB of HBM per device.

```python
import jax
import jax.numpy as jnp
from jax import lax

D = 1024
MH = 24
MP = 64
DS = 128
KC = 4
QH = 8
KVH = 2
HD = 128
FF = 2048
LENGTH = 1024
SEQS = 2
DI = 1536
CX = 1792
SEQ_TOTAL = 16


def draw_segments(key, part):
    key = jax.random.fold_in(key, 7)
    pick_key = jax.random.fold_in(key, 1)
    flag_key = jax.random.fold_in(key, 2)
    shift_key = jax.random.fold_in(key, 3)
    group_count = SEQ_TOTAL // SEQS
    whole_pick = jax.random.randint(pick_key, (group_count,), 0, SEQS)
    sequence_index = jnp.arange(SEQ_TOTAL, dtype=jnp.int32)
    member = sequence_index % SEQS
    chosen = whole_pick[sequence_index // SEQS]
    is_whole = member == chosen
    is_full = member == (chosen + 1) % SEQS
    active = jax.random.randint(flag_key, (SEQ_TOTAL, 2), 0, 2)
    active = jnp.where(is_full[:, None], 1, active)
    active = jnp.where(is_whole[:, None], 0, active)
    cut_reach = LENGTH // 16
    offsets = jax.random.randint(shift_key, (SEQ_TOTAL, 2), -cut_reach, cut_reach + 1)
    cut_points = jnp.arange(1, 3, dtype=jnp.int32) * LENGTH // 3 + offsets
    position = jnp.arange(LENGTH, dtype=jnp.int32)
    crossed = (position[None, :, None] >= cut_points[:, None, :]) & (active[:, None, :] == 1)
    return jnp.sum(crossed.astype(jnp.int32), axis=-1).astype(jnp.int32)


def block_scale(stream_key, dims, shards, smallest, high):
    def one(dim, parts):
        heights = jax.random.uniform(jax.random.fold_in(jax.random.fold_in(stream_key, 6), dim), (parts,), jnp.float32, smallest / len(shards), high / len(shards))
        return jnp.repeat(jnp.exp(heights), dims[dim] // parts).reshape((-1,) + (1,) * (len(dims) - dim - 1))

    factor_of = one(*shards[0])
    for cut in shards[1:]:
        factor_of = factor_of * one(*cut)
    return factor_of


def noise(stream_key, extent, scale, bound, split=(), kind=jnp.bfloat16):
    entries = scale * jax.random.normal(stream_key, extent, jnp.float32)
    if split:
        entries = entries * block_scale(stream_key, extent, split, -0.22, 0.18)
    return jnp.clip(entries, -bound, bound).astype(kind)


def setup_inputs(seed: int = 0) -> dict:
    key_of = jax.random.split(jax.random.key(seed), 23)
    return {
        "tokens": noise(key_of[0], (SEQ_TOTAL, LENGTH, D), 1.0, 6.0, ((0, 8), (1, 4))),
        "segments": draw_segments(jax.random.fold_in(key_of[22], 71), 0),
        "pre_gain": jnp.clip(1.0 + 0.1 * jax.random.normal(key_of[2], (D,), jnp.float32), 0.5, 1.5).astype(jnp.bfloat16),
        "gate_proj": noise(key_of[3], (D, DI), D ** -0.5, 0.1875, ((0, 32),)),
        "mix_proj": noise(key_of[4], (D, CX), D ** -0.5, 0.1875, ((0, 32),)),
        "step_proj": noise(key_of[5], (D, MH), D ** -0.5, 0.1875, ((0, 32),)),
        "conv_taps": noise(key_of[6], (KC, CX), 0.5, 3.0, ((1, 32),)),
        "conv_bias": noise(key_of[7], (CX,), 0.3, 2.0, ((0, 32),)),
        "decay_log": jnp.clip(jax.random.uniform(key_of[8], (MH,), jnp.float32, -7.5, -2.5), -7.5, -2.5),
        "step_bias": jnp.clip(jax.random.uniform(key_of[9], (MH,), jnp.float32, -3.0, -0.5), -3.0, -0.5),
        "skip_scale": jnp.clip(jax.random.uniform(key_of[10], (MH,), jnp.float32, 0.5, 1.5), 0.5, 1.5),
        "inner_gain": jnp.clip(1.0 + 0.1 * jax.random.normal(key_of[11], (DI,), jnp.float32), 0.5, 1.5).astype(jnp.bfloat16),
        "mamba_proj": noise(key_of[12], (DI, D), DI ** -0.5, 0.15625, ((0, 32),)),
        "query_proj": noise(key_of[13], (D, QH * HD), D ** -0.5, 0.1875, ((0, 32),)),
        "key_proj": noise(key_of[14], (D, KVH * HD), D ** -0.5, 0.1875, ((0, 32),)),
        "value_proj": noise(key_of[15], (D, KVH * HD), D ** -0.5, 0.1875, ((0, 32),)),
        "attn_proj": noise(key_of[16], (QH * HD, D), (QH * HD // 16) ** -0.5, 0.75, ((0, 32),)),
        "feed_gain": jnp.clip(1.0 + 0.1 * jax.random.normal(key_of[17], (D,), jnp.float32), 0.5, 1.5).astype(jnp.bfloat16),
        "feed_gate": noise(key_of[18], (D, FF), D ** -0.5, 0.1875, ((0, 32),)),
        "feed_up": noise(key_of[19], (D, FF), D ** -0.5, 0.1875, ((0, 32),)),
        "feed_down": noise(key_of[20], (FF, D), FF ** -0.5, 0.125, ((0, 32),)),
        "cotangent": noise(key_of[21], (SEQ_TOTAL, LENGTH, D), 1.0, 6.0, ((0, 8), (1, 4))),
    }


@jax.custom_vjp
def low(v):
    return lax.optimization_barrier(v.astype(jnp.bfloat16)).astype(jnp.float32)

@jax.custom_vjp
def low_back(v):
    return v

def low_keep(v):
    return (low(v), None)

def low_pass(kept, grad):
    return (grad,)

def back_keep(v):
    return (v, None)

def back_low(kept, grad):
    return (low(grad),)
low.defvjp(low_keep, low_pass)
low_back.defvjp(back_keep, back_low)
epsilon = 1e-05
highest = lax.Precision.HIGHEST
rope_base = 100000000000.0
masked_score = -1e+30

def rms_scale(features):
    return lax.rsqrt(lax.optimization_barrier(jnp.mean(features * features, axis=-1, keepdims=True)) + epsilon)

def gained_norm(features, gain_vec):
    return features * rms_scale(features) * gain_vec

def matmul(left, right):
    return jnp.dot(left, right, precision=highest, preferred_element_type=jnp.float32)

def rotate(features, positions, direction):
    head_size = features.shape[-1]
    half_size = head_size // 2
    freq_exp = lax.broadcasted_iota(jnp.int32, (half_size,), 0).astype(positions.dtype) * (2.0 / head_size)
    inverse = jnp.power(rope_base, -freq_exp)
    angles = positions[:, None] * inverse[None, :]
    cosine = jnp.cos(angles)[:, None, :]
    sine_part = direction * jnp.sin(angles)[:, None, :]
    first_half = features[..., :half_size]
    second_half = features[..., half_size:]
    return jnp.concatenate([first_half * cosine - second_half * sine_part, second_half * cosine + first_half * sine_part], axis=-1)

def conv_local(extended, segment_wide, conv_taps, conv_bias):
    tap_count = conv_taps.shape[0]
    length_now = extended.shape[1] - tap_count + 1
    segment_now = segment_wide[:, tap_count - 1:]
    conv_total = conv_bias
    for offset in range(tap_count):
        window = extended[:, offset:offset + length_now]
        same_doc = (segment_wide[:, offset:offset + length_now] == segment_now)[..., None]
        conv_total = conv_total + conv_taps[offset] * jnp.where(same_doc, window, 0.0)
    return conv_total

def prepare(extended, segment_wide, step_raw, conv_taps, conv_bias, step_bias, decay_log):
    activated = jax.nn.silu(conv_local(extended, segment_wide, conv_taps, conv_bias))
    inner_width = MH * MP
    inner_vals = activated[..., :inner_width].reshape(activated.shape[:-1] + (MH, MP))
    input_map = activated[..., inner_width:inner_width + DS]
    output_map = activated[..., inner_width + DS:]
    step_size = jax.nn.softplus(step_raw + step_bias)
    log_decay = -jnp.exp(decay_log) * step_size
    return (inner_vals, input_map, output_map, step_size, log_decay)

def block_output(step_size, log_decay, inner_vals, input_map, output_map, segment_ids, start_flag, state_in):
    count_rows = log_decay.shape[0]
    cumulative = jnp.cumsum(log_decay, axis=0)
    carried = (jnp.cumsum(start_flag) == 0).astype(cumulative.dtype)
    row_index = lax.broadcasted_iota(jnp.int32, (count_rows, count_rows), 0)
    col_index = lax.broadcasted_iota(jnp.int32, (count_rows, count_rows), 1)
    allowed = ((col_index <= row_index) & (segment_ids[:, None] == segment_ids[None, :]))[:, :, None]
    spread = cumulative[:, None, :] - cumulative[None, :, :]
    mixing = jnp.where(allowed, jnp.exp(jnp.where(allowed, spread, 0.0)), 0.0)
    affinity = jnp.dot(output_map, input_map.T, precision=highest)
    kernel = affinity[:, :, None] * mixing * step_size[None, :, :]
    result = jnp.einsum('ijh,jhp->ihp', kernel, inner_vals, precision=highest)
    entry_scale = carried[:, None] * jnp.exp(cumulative)
    carried_in = jnp.einsum('is,hps->ihp', output_map, state_in, precision=highest)
    return result + entry_scale[:, :, None] * carried_in

def block_summary(step_size, log_decay, inner_vals, input_map, segment_ids, start_flag):
    cumulative = jnp.cumsum(log_decay, axis=0)
    last_cum = cumulative[-1]
    keep_last = (jnp.sum(start_flag) == 0).astype(cumulative.dtype)
    block_decay = keep_last * jnp.exp(last_cum)
    same_last = (segment_ids == segment_ids[-1])[:, None]
    final_weight = jnp.where(same_last, jnp.exp(last_cum[None, :] - cumulative), 0.0) * step_size
    local_state = jnp.einsum('jh,jhp,js->hps', final_weight, inner_vals, input_map, precision=highest)
    return (block_decay, local_state)

def mamba_tail(result, inner_vals, gate_mamba, skip_scale, inner_gain):
    full_out = result + skip_scale[:, None] * inner_vals
    gated_out = full_out.reshape(full_out.shape[:-2] + (MH * MP,)) * jax.nn.silu(gate_mamba)
    return gained_norm(gated_out, inner_gain)

def sequence_mixer(inner_vals, input_map, output_map, step_size, log_decay, segment_ids, start_flag):
    length_all = log_decay.shape[0]
    span_rows = min(128, length_all)
    count_spans = length_all // span_rows

    def to_spans(features):
        return features.reshape((count_spans, span_rows) + features.shape[1:])

    def advance(state, pieces):
        part_inner, part_input, part_output, part_step, part_log, part_segment, part_start = pieces
        result = block_output(part_step, part_log, part_inner, part_input, part_output, part_segment, part_start, state)
        block_decay, local_state = block_summary(part_step, part_log, part_inner, part_input, part_segment, part_start)
        return (block_decay[:, None, None] * state + local_state, result)
    state_zero = jnp.zeros((MH, MP, DS), inner_vals.dtype)
    pieces = (to_spans(inner_vals), to_spans(input_map), to_spans(output_map), to_spans(step_size), to_spans(log_decay), to_spans(segment_ids), to_spans(start_flag))
    _, results = lax.scan(jax.checkpoint(advance), state_zero, pieces)
    return results.reshape(inner_vals.shape)

def sequence_attention(queries, keys_rot, values, segment_ids):
    length_all = queries.shape[0]
    grouped = queries.reshape(length_all, KVH, QH // KVH, HD)
    scores = jnp.einsum('ikgd,jkd->kgij', grouped, keys_rot, precision=highest) * HD ** (-0.5)
    scores = low_back(scores)
    position = lax.broadcasted_iota(jnp.int32, (length_all,), 0)
    allowed = (position[None, :] <= position[:, None]) & (segment_ids[:, None] == segment_ids[None, :])
    scores = jnp.where(allowed, scores, masked_score)
    row_max = lax.optimization_barrier(jnp.max(scores, axis=-1, keepdims=True))
    log_total = row_max + jnp.log(lax.optimization_barrier(jnp.sum(jnp.exp(scores - row_max), axis=-1, keepdims=True)))
    attend = low(jnp.exp(scores - log_total))
    mixed_heads = jnp.einsum('kgij,jkd->ikgd', attend, values, precision=highest)
    return mixed_heads.reshape(length_all, QH * HD)

def full_layer(hidden, segment_ids, start_flag, params):
    pre_gain, gate_proj, mix_proj, step_proj, conv_taps, conv_bias, decay_log, step_bias, skip_scale, inner_gain, mamba_proj, query_proj, key_proj, value_proj, attn_proj, feed_gain, feed_gate, feed_up, feed_down = params
    seq_count, length_all, model_width = hidden.shape
    flat_rows = hidden.reshape(-1, model_width)
    normed = low(gained_norm(flat_rows, pre_gain))
    gate_mamba = low_back(matmul(normed, gate_proj)).reshape(seq_count, length_all, -1)
    conv_input = low_back(matmul(normed, mix_proj)).reshape(seq_count, length_all, -1)
    step_raw = low_back(matmul(normed, step_proj)).reshape(seq_count, length_all, -1)
    tap_count = conv_taps.shape[0]
    extended = jnp.pad(conv_input, ((0, 0), (tap_count - 1, 0), (0, 0)))
    segment_wide = jnp.pad(segment_ids, ((0, 0), (tap_count - 1, 0)))
    inner_vals, input_map, output_map, step_size, log_decay = prepare(extended, segment_wide, step_raw, conv_taps, conv_bias, step_bias, decay_log)
    result = lax.map(jax.checkpoint(lambda pieces: sequence_mixer(*pieces)), (inner_vals, input_map, output_map, step_size, log_decay, segment_ids, start_flag))
    mixed_low = low(mamba_tail(result, inner_vals, gate_mamba, skip_scale, inner_gain))
    branch_mamba = low_back(matmul(mixed_low.reshape(-1, MH * MP), mamba_proj))
    positions = jnp.arange(length_all).astype(hidden.dtype)
    queries = low(rotate(low_back(matmul(normed, query_proj)).reshape(seq_count, length_all, QH, HD), positions, 1.0))
    keys_rot = low(rotate(low_back(matmul(normed, key_proj)).reshape(seq_count, length_all, KVH, HD), positions, 1.0))
    values = low(low_back(matmul(normed, value_proj))).reshape(seq_count, length_all, KVH, HD)
    attended = lax.map(jax.checkpoint(lambda pieces: sequence_attention(*pieces)), (queries, keys_rot, values, segment_ids))
    attended = low(low_back(attended))
    branch_attn = low_back(matmul(attended.reshape(-1, QH * HD), attn_proj))
    residual = flat_rows + branch_mamba + branch_attn
    normed_two = low(gained_norm(residual, feed_gain))
    feed_gate_out = low_back(matmul(normed_two, feed_gate))
    feed_up_out = low_back(matmul(normed_two, feed_up))
    feed_hidden = low(jax.nn.silu(feed_gate_out) * feed_up_out)
    return (residual + matmul(feed_hidden, feed_down)).reshape(seq_count, length_all, model_width)

def reference(tokens, segments, pre_gain, gate_proj, mix_proj, step_proj, conv_taps, conv_bias, decay_log, step_bias, skip_scale, inner_gain, mamba_proj, query_proj, key_proj, value_proj, attn_proj, feed_gain, feed_gate, feed_up, feed_down, cotangent):
    segment_ids = segments.astype(jnp.float32)
    previous = jnp.pad(segment_ids, ((0, 0), (1, 0)))[:, :-1]
    start_flag = (segment_ids != previous).astype(jnp.float32)
    params = tuple((weight_item.astype(jnp.float32) for weight_item in (pre_gain, gate_proj, mix_proj, step_proj, conv_taps, conv_bias, decay_log, step_bias, skip_scale, inner_gain, mamba_proj, query_proj, key_proj, value_proj, attn_proj, feed_gain, feed_gate, feed_up, feed_down)))

    def run_layer(hidden, *weights_all):
        return full_layer(hidden, segment_ids, start_flag, weights_all)
    output, pullback = jax.vjp(run_layer, tokens.astype(jnp.float32), *params)
    gradients = pullback(cotangent.astype(jnp.float32))
    return (output.astype(jnp.bfloat16), gradients[0], gradients[1], gradients[2], gradients[3], gradients[4], gradients[5], gradients[6], gradients[7], gradients[8], gradients[9], gradients[10], gradients[11], gradients[12], gradients[13], gradients[14], gradients[15], gradients[16], gradients[17], gradients[18], gradients[19])
```

```python
import jax
import jax.numpy as jnp
from jax import lax
from jax.sharding import PartitionSpec as P

MH = 24
MP = 64
DS = 128
KC = 4
QH = 8
KVH = 2
HD = 128


epsilon = 1e-05
highest = lax.Precision.HIGHEST
rope_base = 100000000000.0
masked_score = -1e30


def shifted(block, axis, distance):
    devices = range(lax.axis_size(axis))
    route = [(i - distance, i) for i in devices if i - distance in devices]
    return lax.ppermute(block, axis, route)


def index_bits(axis):
    size = lax.axis_size(axis)
    return [(axis, 1 << k) for k in range(size.bit_length() - 1)]


def bit_weight(bit):
    return bit[1] * (lax.axis_size("ctx") if bit[0] == "dp" else 1)


def bit_value(bit):
    return lax.rem(lax.axis_index(bit[0]) // bit[1], 2)


def exchanged(block, bit):
    route = [(i, i ^ bit[1]) for i in range(lax.axis_size(bit[0]))]
    return lax.ppermute(block, bit[0], route)


def halving_order(first_dp):
    ctx_bits, dp_bits = index_bits("ctx"), index_bits("dp")
    if first_dp:
        return ctx_bits[:1] + dp_bits[:1] + ctx_bits[1:] + dp_bits[1:]
    return ctx_bits + dp_bits


def grown(block, order):
    seen = []
    for bit in reversed(order):
        place = sum(bit_weight(b) > bit_weight(bit) for b in seen)
        other = exchanged(block, bit)
        low_half = bit_value(bit) == 0
        block = jnp.stack(
            [jnp.where(low_half, block, other), jnp.where(low_half, other, block)], axis=place
        )
        seen.append(bit)
    return block.reshape((-1,) + block.shape[len(seen) :])


def shrunk(blocks, order):
    left = list(order)
    total = blocks.reshape((2,) * len(left) + blocks.shape[1:])
    for bit in order:
        place = sum(bit_weight(b) > bit_weight(bit) for b in left)
        here = bit_value(bit)
        away = lax.dynamic_index_in_dim(total, 1 - here, place, keepdims=False)
        keep = lax.dynamic_index_in_dim(total, here, place, keepdims=False)
        added = keep.astype(jnp.float32) + exchanged(away, bit).astype(jnp.float32)
        left.remove(bit)
        total = added.astype(jnp.bfloat16) if left else added
    return total


def gather_rows(shard, first_dp):
    return grown(shard, halving_order(first_dp))


def scatter_rows(partial, rows, first_dp):
    return shrunk(partial.reshape((-1, rows) + partial.shape[1:]), halving_order(first_dp))


def butterfly_sum(value):
    for bit in halving_order(False):
        value = value + exchanged(value, bit)
    return value


def prefix(value, axis, combine, identity):
    size, here = (lax.axis_size(axis), lax.axis_index(axis))
    everything = jax.tree.map(
        lambda part, kind: lax.all_gather(part.astype(kind), axis),
        value,
        (jnp.bfloat16, jnp.bfloat16),
    )
    start = jax.tree.map(
        lambda part, zero: jnp.broadcast_to(jnp.asarray(zero, part.dtype), part.shape),
        value,
        identity,
    )

    def prefix_hop(k, before):
        reached = k < here
        new = combine(
            before, jax.tree.map(lambda part, own: part[k].astype(own.dtype), everything, value)
        )
        return jax.tree.map(lambda a, b: jnp.where(reached, a, b), new, before)

    return lax.fori_loop(0, size, prefix_hop, start)


def entering(value, axis, combine, identity):
    size, here = (lax.axis_size(axis), lax.axis_index(axis))
    everything = jax.tree.map(
        lambda part, kind: lax.all_gather(part.astype(kind), axis),
        value,
        jax.tree.map(lambda a: jnp.bfloat16 if a.dtype == jnp.float32 else a.dtype, value),
    )
    start = jax.tree.map(
        lambda part, zero: jnp.broadcast_to(jnp.asarray(zero, part.dtype), part.shape),
        value,
        identity,
    )

    def entering_hop(k, before):
        at = size - 1 - k
        reached = at > here
        new = combine(
            before, jax.tree.map(lambda part, own: part[at].astype(own.dtype), everything, value)
        )
        return jax.tree.map(lambda a, b: jnp.where(reached, a, b), new, before)

    return lax.fori_loop(0, size, entering_hop, start)


def rms_scale(features):
    return lax.rsqrt(jnp.mean(features * features, axis=-1, keepdims=True) + epsilon)


def gained_norm(features, gain_vec):
    return features * rms_scale(features) * gain_vec


def forward_mul(left, right):
    return jnp.dot(left, right, preferred_element_type=jnp.float32)


def outer_sum(left, right):
    return lax.dot_general(
        left, right, (((0,), (0,)), ((), ())), preferred_element_type=jnp.float32
    )


def back_mul(grad_rows, weight):
    return lax.dot_general(
        grad_rows, weight, (((1,), (1,)), ((), ())), preferred_element_type=jnp.float32
    )


def rotate(features, positions, direction):
    head_size = features.shape[-1]
    half_size = head_size // 2
    freq_exp = lax.broadcasted_iota(jnp.int32, (half_size,), 0).astype(positions.dtype) * (
        2.0 / head_size
    )
    inverse = jnp.power(rope_base, -freq_exp)
    angles = positions[:, None] * inverse[None, :]
    cosine = jnp.cos(angles)[:, None, :]
    sine_part = direction * jnp.sin(angles)[:, None, :]
    first_half = features[..., :half_size]
    second_half = features[..., half_size:]
    return jnp.concatenate(
        [
            first_half * cosine - second_half * sine_part,
            second_half * cosine + first_half * sine_part,
        ],
        axis=-1,
    )


def conv_local(extended, segment_wide, conv_taps, conv_bias):
    tap_count = conv_taps.shape[0]
    length_now = extended.shape[1] - tap_count + 1
    segment_now = segment_wide[:, tap_count - 1 :]
    conv_total = conv_bias
    for offset in range(tap_count):
        window = extended[:, offset : offset + length_now]
        same_doc = (segment_wide[:, offset : offset + length_now] == segment_now)[..., None]
        conv_total = conv_total + conv_taps[offset] * jnp.where(same_doc, window, 0.0)
    return conv_total


def prepare(extended, segment_wide, step_raw, conv_taps, conv_bias, step_bias, decay_log):
    activated = jax.nn.silu(conv_local(extended, segment_wide, conv_taps, conv_bias))
    inner_width = MH * MP
    inner_vals = activated[..., :inner_width].reshape(activated.shape[:-1] + (MH, MP))
    input_map = activated[..., inner_width : inner_width + DS]
    output_map = activated[..., inner_width + DS :]
    step_size = jax.nn.softplus(step_raw + step_bias)
    log_decay = -jnp.exp(decay_log) * step_size
    return (inner_vals, input_map, output_map, step_size, log_decay)


def block_output(
    step_size, log_decay, inner_vals, input_map, output_map, segment_ids, start_flag, state_in
):
    count_rows = log_decay.shape[0]
    cumulative = jnp.cumsum(log_decay, axis=0)
    carried = (jnp.cumsum(start_flag) == 0).astype(cumulative.dtype)
    row_index = lax.broadcasted_iota(jnp.int32, (count_rows, count_rows), 0)
    col_index = lax.broadcasted_iota(jnp.int32, (count_rows, count_rows), 1)
    allowed = ((col_index <= row_index) & (segment_ids[:, None] == segment_ids[None, :]))[
        :, :, None
    ]
    spread = cumulative[:, None, :] - cumulative[None, :, :]
    mixing = jnp.where(allowed, jnp.exp(jnp.where(allowed, spread, 0.0)), 0.0)
    affinity = jnp.dot(output_map, input_map.T, precision=highest)
    kernel = affinity[:, :, None] * mixing * step_size[None, :, :]
    result = jnp.einsum("ijh,jhp->ihp", kernel, inner_vals, precision=highest)
    entry_scale = carried[:, None] * jnp.exp(cumulative)
    carried_in = jnp.einsum("is,hps->ihp", output_map, state_in, precision=highest)
    return result + entry_scale[:, :, None] * carried_in


def block_summary(step_size, log_decay, inner_vals, input_map, segment_ids, start_flag):
    cumulative = jnp.cumsum(log_decay, axis=0)
    last_cum = cumulative[-1]
    keep_last = (jnp.sum(start_flag) == 0).astype(cumulative.dtype)
    block_decay = keep_last * jnp.exp(last_cum)
    same_last = (segment_ids == segment_ids[-1])[:, None]
    final_weight = jnp.where(same_last, jnp.exp(last_cum[None, :] - cumulative), 0.0) * step_size
    local_state = jnp.einsum(
        "jh,jhp,js->hps", final_weight, inner_vals, input_map, precision=highest
    )
    return (block_decay, local_state)


def mamba_tail(result, inner_vals, gate_mamba, skip_scale, inner_gain):
    full_out = result + skip_scale[:, None] * inner_vals
    gated_out = full_out.reshape(full_out.shape[:-2] + (MH * MP,)) * jax.nn.silu(gate_mamba)
    return gained_norm(gated_out, inner_gain)


def chain_combine(earlier, later):
    return (earlier[0] * later[0], later[0][..., None, None] * earlier[1] + later[1])


def attention_mask(positions, segment_ids, segment_all):
    key_count = segment_all.shape[1]
    key_pos = lax.broadcasted_iota(jnp.int32, (key_count,), 0).astype(jnp.float32)
    causal = key_pos[None, :] <= positions[:, None]
    same_doc = segment_ids[:, :, None] == segment_all[:, None, :]
    return (causal[None] & same_doc)[:, None, None]


def score_block(grouped, keys_all, allowed):
    scores = jnp.einsum(
        "sikgd,sjkd->skgij", grouped, keys_all, preferred_element_type=jnp.float32
    ) * HD ** (-0.5)
    return jnp.where(allowed, scores, masked_score)


def body(
    tokens,
    segments,
    pre_gain,
    gate_proj,
    mix_proj,
    step_proj,
    conv_taps,
    conv_bias,
    decay_log,
    step_bias,
    skip_scale,
    inner_gain,
    mamba_proj,
    query_proj,
    key_proj,
    value_proj,
    attn_proj,
    feed_gain,
    feed_gate,
    feed_up,
    feed_down,
    cotangent,
):
    shard_rows = gate_proj.shape[0]
    inner_rows = mamba_proj.shape[0]
    attn_rows = attn_proj.shape[0]
    feat_rows = conv_bias.shape[0]
    down_rows = feed_down.shape[0]
    small_parts = (pre_gain, feed_gain, inner_gain, conv_bias, conv_taps.reshape(-1))
    small = jnp.concatenate(small_parts)
    small = jnp.pad(small, (0, shard_rows * 16 - small.shape[0])).reshape(shard_rows, 16)
    step_block = jnp.pad(jnp.concatenate([step_proj, small], axis=1), ((0, 0), (0, 128 - MH - 16)))
    pack_two = gather_rows(
        jnp.concatenate([mix_proj, key_proj, value_proj, step_block], axis=1), True
    ).reshape(-1, 2304 + 128)
    pack_one = gather_rows(jnp.concatenate([gate_proj, query_proj], axis=1), False).reshape(
        -1, 2560
    )
    pack_mix = gather_rows(jnp.concatenate([mamba_proj, attn_proj], axis=0), True)
    mamba_whole = pack_mix[:, :inner_rows].reshape(-1, pack_mix.shape[-1])
    attn_whole = pack_mix[:, inner_rows:].reshape(-1, pack_mix.shape[-1])
    gate_whole = gather_rows(feed_gate, False).reshape(-1, feed_gate.shape[1])
    up_whole = gather_rows(feed_up, True).reshape(-1, feed_up.shape[1])
    down_whole = gather_rows(feed_down, False).reshape(-1, feed_down.shape[1])
    small_all = pack_two[:, 2304 + MH : 2304 + MH + 16].reshape(-1, shard_rows * 16)
    cuts = [0]
    for part in small_parts:
        cuts.append(cuts[-1] + part.shape[0])
    pre_whole, feed_whole, inner_whole, bias_whole = (
        small_all[:, cuts[k] : cuts[k + 1]].reshape(-1).astype(jnp.float32) for k in range(4)
    )
    taps_float = (
        small_all[:, cuts[4] : cuts[5]]
        .reshape(-1, KC, feat_rows)
        .transpose(1, 0, 2)
        .reshape(KC, -1)
        .astype(jnp.float32)
    )
    seq_count, block_rows, model_width = tokens.shape
    tap_count = KC
    inner_width = MH * MP
    group_size = QH // KVH
    ctx_index = lax.axis_index("ctx")
    flat_rows = tokens.reshape(seq_count * block_rows, model_width).astype(jnp.float32)
    normed = gained_norm(flat_rows, pre_whole).astype(jnp.bfloat16)
    front_one = forward_mul(normed, pack_one)
    front_two = forward_mul(normed, pack_two)
    gate_mamba = front_one[:, :inner_width].reshape(seq_count, block_rows, inner_width)
    conv_input = front_two[:, :1792].reshape(seq_count, block_rows, -1)
    step_raw = front_two[:, 2304 : 2304 + MH].reshape(seq_count, block_rows, MH)
    segment_ids = segments.astype(jnp.float32)
    prev_rows, prev_segment = shifted(
        (conv_input[:, block_rows - tap_count + 1 :], segment_ids[:, block_rows - tap_count + 1 :]),
        "ctx",
        1,
    )
    extended = jnp.concatenate([prev_rows, conv_input], axis=1)
    segment_wide = jnp.concatenate([prev_segment, segment_ids], axis=1)
    start_flag = (
        segment_ids != segment_wide[:, tap_count - 2 : tap_count - 2 + block_rows]
    ).astype(jnp.float32)
    prepared, prepare_back = jax.vjp(
        lambda *rest: prepare(rest[0], segment_wide, *rest[1:]),
        extended,
        step_raw,
        taps_float,
        bias_whole,
        step_bias,
        decay_log,
    )
    inner_vals, input_map, output_map, step_size, log_decay = prepared
    (block_decay, local_state), summary_back = jax.vjp(
        lambda step_in, log_in, inner_in, input_in: jax.vmap(block_summary)(
            step_in, log_in, inner_in, input_in, segment_ids, start_flag
        ),
        step_size,
        log_decay,
        inner_vals,
        input_map,
    )
    identity_pair = (jnp.ones_like(block_decay), jnp.zeros_like(local_state))
    carried = prefix((block_decay, local_state), "ctx", chain_combine, identity_pair)
    state_in = carried[1]
    def mamba_front(step_in, log_in, inner_in, input_in, output_in, state_arg, gate_in, skip_in, gain_in):
        result_in = jax.vmap(block_output)(
            step_in, log_in, inner_in, input_in, output_in, segment_ids, start_flag, state_arg
        )
        return mamba_tail(result_in, inner_in, gate_in, skip_in, gain_in)

    mixed, front_back = jax.vjp(
        mamba_front,
        step_size,
        log_decay,
        inner_vals,
        input_map,
        output_map,
        state_in,
        gate_mamba,
        skip_scale,
        inner_whole,
    )
    mixed_low = mixed.astype(jnp.bfloat16)
    branch_mamba = forward_mul(mixed_low.reshape(-1, inner_width), mamba_whole)
    positions = (ctx_index * block_rows + lax.broadcasted_iota(jnp.int32, (block_rows,), 0)).astype(
        jnp.float32
    )
    query_pre = front_one[:, inner_width:].reshape(seq_count, block_rows, QH, HD)
    key_pre = front_two[:, 1792:2048].reshape(seq_count, block_rows, KVH, HD)
    value_pre = front_two[:, 2048:2304].reshape(seq_count, block_rows, KVH, HD)
    queries = rotate(query_pre, positions, 1.0).astype(jnp.bfloat16)
    keys_rot = rotate(key_pre, positions, 1.0).astype(jnp.bfloat16)
    values = value_pre.astype(jnp.bfloat16)
    ctx_size = lax.axis_size("ctx")
    ctx_order = index_bits("ctx")
    both = grown(jnp.concatenate([keys_rot, values], axis=2), ctx_order)
    both = both.transpose(1, 0, 2, 3, 4).reshape(seq_count, -1, 2 * KVH, HD)
    keys_all, values_all = both[:, :, :KVH], both[:, :, KVH:]
    segment_all = grown(segment_ids.astype(jnp.bfloat16), ctx_order)
    segment_all = segment_all.transpose(1, 0, 2).reshape(seq_count, -1)
    grouped = queries.reshape(seq_count, block_rows, KVH, group_size, HD)
    allowed = attention_mask(positions, segment_ids, segment_all.astype(jnp.float32))
    scores = score_block(grouped, keys_all, allowed)
    row_max = jnp.max(scores, axis=-1, keepdims=True)
    log_total = row_max + jnp.log(jnp.sum(jnp.exp(scores - row_max), axis=-1, keepdims=True))
    attend = jnp.exp(scores - log_total).astype(jnp.bfloat16)
    attended = jnp.einsum(
        "skgij,sjkd->sikgd", attend, values_all, preferred_element_type=jnp.float32
    ).astype(jnp.bfloat16)
    branch_attn = forward_mul(attended.reshape(-1, QH * HD), attn_whole)
    residual = flat_rows + branch_mamba + branch_attn
    feed_scale = feed_whole
    normed_two = gained_norm(residual, feed_scale).astype(jnp.bfloat16)
    feed_gate_out = forward_mul(normed_two, gate_whole)
    feed_up_out = forward_mul(normed_two, up_whole)
    feed_hidden = (jax.nn.silu(feed_gate_out) * feed_up_out).astype(jnp.bfloat16)
    output = (
        (residual + forward_mul(feed_hidden, down_whole))
        .astype(jnp.bfloat16)
        .reshape(seq_count, block_rows, model_width)
    )
    upstream = cotangent.reshape(-1, model_width)
    grad_feed_down = outer_sum(feed_hidden, upstream)
    grad_hidden = back_mul(upstream, down_whole)
    _, swiglu_back = jax.vjp(
        lambda gate_arg, up_arg: jax.nn.silu(gate_arg) * up_arg, feed_gate_out, feed_up_out
    )
    grad_gate_ff, grad_up_ff = swiglu_back(grad_hidden)
    gate_ff_low = grad_gate_ff.astype(jnp.bfloat16)
    up_ff_low = grad_up_ff.astype(jnp.bfloat16)
    grad_feed_gate = outer_sum(normed_two, gate_ff_low)
    grad_feed_up = outer_sum(normed_two, up_ff_low)
    grad_normed_two = back_mul(gate_ff_low, gate_whole) + back_mul(
        up_ff_low, up_whole
    )
    _, norm_two_back = jax.vjp(gained_norm, residual, feed_whole)
    grad_res_norm, grad_feed_gain = norm_two_back(grad_normed_two)
    grad_residual = upstream.astype(jnp.float32) + grad_res_norm
    residual_low = grad_residual.astype(jnp.bfloat16)
    grad_mamba_proj = outer_sum(mixed_low.reshape(-1, inner_width), residual_low)
    grad_attn_proj = outer_sum(attended.reshape(-1, QH * HD), residual_low)
    grad_mixed = back_mul(residual_low, mamba_whole).reshape(
        seq_count, block_rows, inner_width
    )
    grad_attended = (
        back_mul(residual_low, attn_whole)
        .astype(jnp.bfloat16)
        .reshape(seq_count, block_rows, KVH, group_size, HD)
    )
    scores_again = score_block(grouped, keys_all, allowed)
    attend_full = jnp.exp(scores_again - log_total)
    attend_again = attend_full.astype(jnp.bfloat16)
    grad_attend = jnp.einsum(
        "sikgd,sjkd->skgij", grad_attended, values_all, preferred_element_type=jnp.float32
    )
    grad_values_all = jnp.einsum(
        "skgij,sikgd->sjkd", attend_again, grad_attended, preferred_element_type=jnp.float32
    )
    row_dot = jnp.sum(attend_full * grad_attend, axis=-1, keepdims=True)
    grad_scores = (attend_full * (grad_attend - row_dot)).astype(jnp.bfloat16)
    grad_queries = jnp.einsum(
        "skgij,sjkd->sikgd", grad_scores, keys_all, preferred_element_type=jnp.float32
    ) * HD ** (-0.5)
    grad_keys_all = jnp.einsum(
        "skgij,sikgd->sjkd", grad_scores, grouped, preferred_element_type=jnp.float32
    ) * HD ** (-0.5)
    grad_both = jnp.concatenate([grad_keys_all, grad_values_all], axis=2).astype(jnp.bfloat16)
    grad_both = grad_both.reshape(seq_count, ctx_size, block_rows, 2 * KVH, HD)
    grad_both = shrunk(grad_both.transpose(1, 0, 2, 3, 4), ctx_order)
    grad_keys, grad_values = grad_both[:, :, :KVH], grad_both[:, :, KVH:]
    query_low = (
        rotate(grad_queries.reshape(seq_count, block_rows, QH, HD), positions, -1.0)
        .astype(jnp.bfloat16)
        .reshape(-1, QH * HD)
    )
    key_low = rotate(grad_keys, positions, -1.0).astype(jnp.bfloat16).reshape(-1, KVH * HD)
    value_low = grad_values.astype(jnp.bfloat16).reshape(-1, KVH * HD)
    front_grads = front_back(grad_mixed)
    chain_grads = entering((block_decay, front_grads[5]), "ctx", chain_combine, identity_pair)
    grad_state_out = chain_grads[1]
    grad_decay = jnp.sum(grad_state_out * state_in, axis=(2, 3))
    summary_grads = summary_back((grad_decay, grad_state_out))
    (
        grad_extended,
        grad_step_raw,
        grad_conv_taps,
        grad_conv_bias,
        grad_step_bias,
        grad_decay_log,
    ) = prepare_back(
        (
            front_grads[2] + summary_grads[2],
            front_grads[3] + summary_grads[3],
            front_grads[4],
            front_grads[0] + summary_grads[0],
            front_grads[1] + summary_grads[1],
        )
    )
    back_rows = shifted(grad_extended[:, : tap_count - 1].astype(jnp.bfloat16), "ctx", -1).astype(
        jnp.float32
    )
    grad_conv_input = (
        grad_extended[:, tap_count - 1 :].at[:, block_rows - tap_count + 1 :].add(back_rows)
    )
    gate_low = front_grads[6].astype(jnp.bfloat16).reshape(-1, inner_width)
    conv_low = grad_conv_input.astype(jnp.bfloat16).reshape(-1, grad_conv_input.shape[-1])
    step_low = grad_step_raw.astype(jnp.bfloat16).reshape(-1, MH)
    lows_one = jnp.concatenate([gate_low, query_low], axis=1)
    lows_two = jnp.concatenate([conv_low, key_low, value_low], axis=1)
    step_wide = jnp.pad(step_low, ((0, 0), (0, 128 - MH)))
    grad_one = outer_sum(normed, lows_one)
    grad_two = outer_sum(normed, lows_two)
    grad_step = outer_sum(normed, step_low)
    grad_normed = back_mul(lows_one, pack_one) + back_mul(
        jnp.concatenate([lows_two, step_wide], axis=1), pack_two
    )
    _, norm_one_back = jax.vjp(gained_norm, flat_rows, pre_whole)
    grad_flat, grad_pre_gain = norm_one_back(grad_normed)
    grad_tokens = (grad_residual + grad_flat).reshape(seq_count, block_rows, model_width)
    device_count = lax.axis_size("dp") * ctx_size
    small_grads = jnp.concatenate(
        [
            grad_pre_gain.reshape(device_count, -1),
            grad_feed_gain.reshape(device_count, -1),
            front_grads[8].reshape(device_count, -1),
            grad_conv_bias.reshape(device_count, -1),
            grad_conv_taps.reshape(KC, device_count, -1)
            .transpose(1, 0, 2)
            .reshape(device_count, -1),
        ],
        axis=1,
    )
    small_grads = jnp.pad(
        small_grads, ((0, 0), (0, shard_rows * 16 - small_grads.shape[1]))
    ).reshape(-1, 16)
    step_grads = jnp.pad(
        jnp.concatenate([grad_step, small_grads], axis=1), ((0, 0), (0, 128 - MH - 16))
    )
    low = jnp.bfloat16
    own_down = scatter_rows(grad_feed_down.astype(low), down_rows, False)
    own_gate = scatter_rows(grad_feed_gate.astype(low), shard_rows, False)
    own_up = scatter_rows(grad_feed_up.astype(low), shard_rows, True)
    own_mix = scatter_rows(
        jnp.concatenate(
            [
                grad_mamba_proj.astype(low).reshape(device_count, inner_rows, -1),
                grad_attn_proj.astype(low).reshape(device_count, attn_rows, -1),
            ],
            axis=1,
        ).reshape(device_count * (inner_rows + attn_rows), -1),
        inner_rows + attn_rows,
        True,
    )
    own_one = scatter_rows(grad_one.astype(low), shard_rows, False)
    own_two = scatter_rows(
        jnp.concatenate([grad_two.astype(low), step_grads.astype(low)], axis=1), shard_rows, True
    )
    own_small = own_two[:, 2304 + MH : 2304 + MH + 16].reshape(-1)
    head_sums = butterfly_sum(jnp.stack([grad_decay_log, grad_step_bias, front_grads[7]]))
    return (
        output,
        grad_tokens,
        own_small[cuts[0] : cuts[1]],
        own_one[:, :inner_width],
        own_two[:, :1792],
        own_two[:, 2304 : 2304 + MH],
        own_small[cuts[4] : cuts[5]].reshape(KC, feat_rows),
        own_small[cuts[3] : cuts[4]],
        head_sums[0],
        head_sums[1],
        head_sums[2],
        own_small[cuts[2] : cuts[3]],
        own_mix[:inner_rows],
        own_one[:, inner_width:],
        own_two[:, 1792:2048],
        own_two[:, 2048:2304],
        own_mix[inner_rows:],
        own_small[cuts[1] : cuts[2]],
        own_gate,
        own_up,
        own_down,
    )


def solution(mesh):
    return jax.shard_map(
        body,
        mesh=mesh,
        in_specs=(
            P("dp", "ctx", None),
            P("dp", "ctx"),
            P(("dp", "ctx")),
            P(("dp", "ctx"), None),
            P(("dp", "ctx"), None),
            P(("dp", "ctx"), None),
            P(None, ("dp", "ctx")),
            P(("dp", "ctx")),
            P(),
            P(),
            P(),
            P(("dp", "ctx")),
            P(("dp", "ctx"), None),
            P(("dp", "ctx"), None),
            P(("dp", "ctx"), None),
            P(("dp", "ctx"), None),
            P(("dp", "ctx"), None),
            P(("dp", "ctx")),
            P(("dp", "ctx"), None),
            P(("dp", "ctx"), None),
            P(("dp", "ctx"), None),
            P("dp", "ctx", None),
        ),
        out_specs=(
            P("dp", "ctx", None),
            P("dp", "ctx", None),
            P(("dp", "ctx")),
            P(("dp", "ctx"), None),
            P(("dp", "ctx"), None),
            P(("dp", "ctx"), None),
            P(None, ("dp", "ctx")),
            P(("dp", "ctx")),
            P(),
            P(),
            P(),
            P(("dp", "ctx")),
            P(("dp", "ctx"), None),
            P(("dp", "ctx"), None),
            P(("dp", "ctx"), None),
            P(("dp", "ctx"), None),
            P(("dp", "ctx"), None),
            P(("dp", "ctx")),
            P(("dp", "ctx"), None),
            P(("dp", "ctx"), None),
            P(("dp", "ctx"), None),
        ),
        check_vma=False,
    )
```

```python
import jax
import jax.numpy as jnp
from jax import lax
from jax.sharding import PartitionSpec as P

MH = 24
MP = 64
DS = 128
KC = 4
QH = 8
KVH = 2
HD = 128


epsilon = 1e-05
highest = lax.Precision.HIGH
rope_base = 100000000000.0
masked_score = -1e30


def shifted(block, axis, distance):
    devices = range(lax.axis_size(axis))
    route = [(i - distance, i) for i in devices if i - distance in devices]
    return lax.ppermute(block, axis, route)


def index_bits(axis):
    size = lax.axis_size(axis)
    return [(axis, 1 << k) for k in range(size.bit_length() - 1)]


def bit_weight(bit):
    return bit[1] * (lax.axis_size("ctx") if bit[0] == "dp" else 1)


def bit_value(bit):
    return lax.rem(lax.axis_index(bit[0]) // bit[1], 2)


def exchanged(block, bit):
    route = [(i, i ^ bit[1]) for i in range(lax.axis_size(bit[0]))]
    return lax.ppermute(block, bit[0], route)


def halving_order(first_dp):
    ctx_bits, dp_bits = index_bits("ctx"), index_bits("dp")
    if first_dp:
        return ctx_bits[:1] + dp_bits[:1] + ctx_bits[1:] + dp_bits[1:]
    return ctx_bits + dp_bits


def grown(block, order):
    seen = []
    for bit in reversed(order):
        place = sum(bit_weight(b) > bit_weight(bit) for b in seen)
        other = exchanged(block, bit)
        low_half = bit_value(bit) == 0
        block = jnp.stack(
            [jnp.where(low_half, block, other), jnp.where(low_half, other, block)], axis=place
        )
        seen.append(bit)
    return block.reshape((-1,) + block.shape[len(seen) :])


def shrunk(blocks, order, gates=()):
    left = list(order)
    total = blocks.reshape((2,) * len(left) + blocks.shape[1:])
    for stage, bit in enumerate(order):
        place = sum(bit_weight(b) > bit_weight(bit) for b in left)
        here = bit_value(bit)
        away = lax.dynamic_index_in_dim(total, 1 - here, place, keepdims=False)
        keep = lax.dynamic_index_in_dim(total, here, place, keepdims=False)
        added = keep.astype(jnp.float32) + exchanged(away, bit).astype(jnp.float32)
        left.remove(bit)
        total = added.astype(jnp.bfloat16) if left else added
        if stage < len(gates) and gates[stage] is not None:
            total, _ = lax.optimization_barrier((total, gates[stage]))
    return total


def gather_rows(shard, first_dp):
    return grown(shard, halving_order(first_dp))


def scatter_rows(partial, rows, first_dp, gates=()):
    return shrunk(partial.reshape((-1, rows) + partial.shape[1:]), halving_order(first_dp), gates)


def butterfly_sum(value):
    for bit in halving_order(False):
        value = value + exchanged(value, bit)
    return value


def prefix(value, axis, combine, identity):
    size, here = (lax.axis_size(axis), lax.axis_index(axis))
    everything = jax.tree.map(
        lambda part, kind: lax.all_gather(part.astype(kind), axis),
        value,
        (jnp.bfloat16, jnp.bfloat16),
    )
    start = jax.tree.map(
        lambda part, zero: jnp.broadcast_to(jnp.asarray(zero, part.dtype), part.shape),
        value,
        identity,
    )

    def prefix_hop(k, before):
        reached = k < here
        new = combine(
            before, jax.tree.map(lambda part, own: part[k].astype(own.dtype), everything, value)
        )
        return jax.tree.map(lambda a, b: jnp.where(reached, a, b), new, before)

    return lax.fori_loop(0, size, prefix_hop, start)


def entering(value, axis, combine, identity):
    size, here = (lax.axis_size(axis), lax.axis_index(axis))
    everything = jax.tree.map(
        lambda part, kind: lax.all_gather(part.astype(kind), axis),
        value,
        jax.tree.map(lambda a: jnp.bfloat16 if a.dtype == jnp.float32 else a.dtype, value),
    )
    start = jax.tree.map(
        lambda part, zero: jnp.broadcast_to(jnp.asarray(zero, part.dtype), part.shape),
        value,
        identity,
    )

    def entering_hop(k, before):
        at = size - 1 - k
        reached = at > here
        new = combine(
            before, jax.tree.map(lambda part, own: part[at].astype(own.dtype), everything, value)
        )
        return jax.tree.map(lambda a, b: jnp.where(reached, a, b), new, before)

    return lax.fori_loop(0, size, entering_hop, start)


def rms_scale(features):
    return lax.rsqrt(jnp.mean(features * features, axis=-1, keepdims=True) + epsilon)


def gained_norm(features, gain_vec):
    return features * rms_scale(features) * gain_vec


def forward_mul(left, right):
    return jnp.dot(left, right, preferred_element_type=jnp.float32)


def outer_sum(left, right):
    return lax.dot_general(
        left, right, (((0,), (0,)), ((), ())), preferred_element_type=jnp.float32
    )


def back_mul(grad_rows, weight):
    return lax.dot_general(
        grad_rows, weight, (((1,), (1,)), ((), ())), preferred_element_type=jnp.float32
    )


def rotate(features, positions, direction):
    head_size = features.shape[-1]
    half_size = head_size // 2
    freq_exp = lax.broadcasted_iota(jnp.int32, (half_size,), 0).astype(positions.dtype) * (
        2.0 / head_size
    )
    inverse = jnp.power(rope_base, -freq_exp)
    angles = positions[:, None] * inverse[None, :]
    cosine = jnp.cos(angles)[:, None, :]
    sine_part = direction * jnp.sin(angles)[:, None, :]
    first_half = features[..., :half_size]
    second_half = features[..., half_size:]
    return jnp.concatenate(
        [
            first_half * cosine - second_half * sine_part,
            second_half * cosine + first_half * sine_part,
        ],
        axis=-1,
    )


def conv_local(extended, segment_wide, conv_taps, conv_bias):
    tap_count = conv_taps.shape[0]
    length_now = extended.shape[1] - tap_count + 1
    segment_now = segment_wide[:, tap_count - 1 :]
    conv_total = conv_bias
    for offset in range(tap_count):
        window = extended[:, offset : offset + length_now]
        same_doc = (segment_wide[:, offset : offset + length_now] == segment_now)[..., None]
        conv_total = conv_total + conv_taps[offset] * jnp.where(same_doc, window, 0.0)
    return conv_total


def prepare(extended, segment_wide, step_raw, conv_taps, conv_bias, step_bias, decay_log):
    activated = jax.nn.silu(conv_local(extended, segment_wide, conv_taps, conv_bias))
    inner_width = MH * MP
    inner_vals = activated[..., :inner_width].reshape(activated.shape[:-1] + (MH, MP))
    input_map = activated[..., inner_width : inner_width + DS]
    output_map = activated[..., inner_width + DS :]
    step_size = jax.nn.softplus(step_raw + step_bias)
    log_decay = -jnp.exp(decay_log) * step_size
    return (inner_vals, input_map, output_map, step_size, log_decay)


def block_output(
    step_size, log_decay, inner_vals, input_map, output_map, segment_ids, start_flag, state_in
):
    count_rows = log_decay.shape[0]
    cumulative = jnp.cumsum(log_decay, axis=0)
    carried = (jnp.cumsum(start_flag) == 0).astype(cumulative.dtype)
    row_index = lax.broadcasted_iota(jnp.int32, (count_rows, count_rows), 0)
    col_index = lax.broadcasted_iota(jnp.int32, (count_rows, count_rows), 1)
    allowed = ((col_index <= row_index) & (segment_ids[:, None] == segment_ids[None, :]))[
        :, :, None
    ]
    spread = cumulative[:, None, :] - cumulative[None, :, :]
    mixing = jnp.where(allowed, jnp.exp(jnp.where(allowed, spread, 0.0)), 0.0)
    affinity = jnp.dot(output_map, input_map.T, precision=highest)
    kernel = affinity[:, :, None] * mixing * step_size[None, :, :]
    result = jnp.einsum("ijh,jhp->ihp", kernel, inner_vals, precision=highest)
    entry_scale = carried[:, None] * jnp.exp(cumulative)
    carried_in = jnp.einsum("is,hps->ihp", output_map, state_in, precision=highest)
    return result + entry_scale[:, :, None] * carried_in


def block_summary(step_size, log_decay, inner_vals, input_map, segment_ids, start_flag):
    cumulative = jnp.cumsum(log_decay, axis=0)
    last_cum = cumulative[-1]
    keep_last = (jnp.sum(start_flag) == 0).astype(cumulative.dtype)
    block_decay = keep_last * jnp.exp(last_cum)
    same_last = (segment_ids == segment_ids[-1])[:, None]
    final_weight = jnp.where(same_last, jnp.exp(last_cum[None, :] - cumulative), 0.0) * step_size
    local_state = jnp.einsum(
        "jh,jhp,js->hps", final_weight, inner_vals, input_map, precision=highest
    )
    return (block_decay, local_state)


def mamba_tail(result, inner_vals, gate_mamba, skip_scale, inner_gain):
    full_out = result + skip_scale[:, None] * inner_vals
    gated_out = full_out.reshape(full_out.shape[:-2] + (MH * MP,)) * jax.nn.silu(gate_mamba)
    return gained_norm(gated_out, inner_gain)


def chain_combine(earlier, later):
    return (earlier[0] * later[0], later[0][..., None, None] * earlier[1] + later[1])


def attention_mask(positions, segment_ids, segment_all):
    key_count = segment_all.shape[1]
    key_pos = lax.broadcasted_iota(jnp.int32, (key_count,), 0).astype(jnp.float32)
    causal = key_pos[None, :] <= positions[:, None]
    same_doc = segment_ids[:, :, None] == segment_all[:, None, :]
    return (causal[None] & same_doc)[:, None, None]


def score_block(grouped, keys_all, allowed):
    scores = jnp.einsum(
        "sikgd,sjkd->skgij", grouped, keys_all, preferred_element_type=jnp.float32
    ) * HD ** (-0.5)
    return jnp.where(allowed, scores, masked_score)


def body(
    tokens,
    segments,
    pre_gain,
    gate_proj,
    mix_proj,
    step_proj,
    conv_taps,
    conv_bias,
    decay_log,
    step_bias,
    skip_scale,
    inner_gain,
    mamba_proj,
    query_proj,
    key_proj,
    value_proj,
    attn_proj,
    feed_gain,
    feed_gate,
    feed_up,
    feed_down,
    cotangent,
):
    shard_rows = gate_proj.shape[0]
    inner_rows = mamba_proj.shape[0]
    attn_rows = attn_proj.shape[0]
    feat_rows = conv_bias.shape[0]
    down_rows = feed_down.shape[0]
    small_parts = (pre_gain, feed_gain, inner_gain, conv_bias, conv_taps.reshape(-1))
    small = jnp.concatenate(small_parts)
    small = jnp.pad(small, (0, shard_rows * 16 - small.shape[0])).reshape(shard_rows, 16)
    step_block = jnp.pad(jnp.concatenate([step_proj, small], axis=1), ((0, 0), (0, 128 - MH - 16)))
    pack_two = gather_rows(
        jnp.concatenate([mix_proj, key_proj, value_proj, step_block], axis=1), True
    ).reshape(-1, 2304 + 128)
    pack_one = gather_rows(jnp.concatenate([gate_proj, query_proj], axis=1), False).reshape(
        -1, 2560
    )
    mamba_proj, attn_proj, feed_gate, feed_up, feed_down, pack_one, pack_two = (
        lax.optimization_barrier(
            (mamba_proj, attn_proj, feed_gate, feed_up, feed_down, pack_one, pack_two)
        )
    )
    pack_mix = gather_rows(jnp.concatenate([mamba_proj, attn_proj], axis=0), True)
    mamba_whole = pack_mix[:, :inner_rows].reshape(-1, pack_mix.shape[-1])
    attn_whole = pack_mix[:, inner_rows:].reshape(-1, pack_mix.shape[-1])
    gate_whole = gather_rows(feed_gate, False).reshape(-1, feed_gate.shape[1])
    up_whole = gather_rows(feed_up, True).reshape(-1, feed_up.shape[1])
    down_whole = gather_rows(feed_down, False).reshape(-1, feed_down.shape[1])
    small_all = pack_two[:, 2304 + MH : 2304 + MH + 16].reshape(-1, shard_rows * 16)
    cuts = [0]
    for part in small_parts:
        cuts.append(cuts[-1] + part.shape[0])
    pre_whole, feed_whole, inner_whole, bias_whole = (
        small_all[:, cuts[k] : cuts[k + 1]].reshape(-1).astype(jnp.float32) for k in range(4)
    )
    taps_float = (
        small_all[:, cuts[4] : cuts[5]]
        .reshape(-1, KC, feat_rows)
        .transpose(1, 0, 2)
        .reshape(KC, -1)
        .astype(jnp.float32)
    )
    seq_count, block_rows, model_width = tokens.shape
    tap_count = KC
    inner_width = MH * MP
    group_size = QH // KVH
    ctx_index = lax.axis_index("ctx")
    flat_rows = tokens.reshape(seq_count * block_rows, model_width).astype(jnp.float32)
    normed = gained_norm(flat_rows, pre_whole).astype(jnp.bfloat16)
    front_one = forward_mul(normed, pack_one)
    front_two = forward_mul(normed, pack_two)
    gate_mamba = front_one[:, :inner_width].reshape(seq_count, block_rows, inner_width)
    conv_input = front_two[:, :1792].reshape(seq_count, block_rows, -1)
    step_raw = front_two[:, 2304 : 2304 + MH].reshape(seq_count, block_rows, MH)
    segment_ids = segments.astype(jnp.float32)
    prev_rows, prev_segment = shifted(
        (conv_input[:, block_rows - tap_count + 1 :], segment_ids[:, block_rows - tap_count + 1 :]),
        "ctx",
        1,
    )
    extended = jnp.concatenate([prev_rows, conv_input], axis=1)
    segment_wide = jnp.concatenate([prev_segment, segment_ids], axis=1)
    start_flag = (
        segment_ids != segment_wide[:, tap_count - 2 : tap_count - 2 + block_rows]
    ).astype(jnp.float32)
    prepared, prepare_back = jax.vjp(
        lambda *rest: prepare(rest[0], segment_wide, *rest[1:]),
        extended,
        step_raw,
        taps_float,
        bias_whole,
        step_bias,
        decay_log,
    )
    inner_vals, input_map, output_map, step_size, log_decay = prepared
    (block_decay, local_state), summary_back = jax.vjp(
        lambda step_in, log_in, inner_in, input_in: jax.vmap(block_summary)(
            step_in, log_in, inner_in, input_in, segment_ids, start_flag
        ),
        step_size,
        log_decay,
        inner_vals,
        input_map,
    )
    identity_pair = (jnp.ones_like(block_decay), jnp.zeros_like(local_state))
    carried = prefix((block_decay, local_state), "ctx", chain_combine, identity_pair)
    state_in = carried[1]
    def mamba_front(step_in, log_in, inner_in, input_in, output_in, state_arg, gate_in, skip_in, gain_in):
        result_in = jax.vmap(block_output)(
            step_in, log_in, inner_in, input_in, output_in, segment_ids, start_flag, state_arg
        )
        return mamba_tail(result_in, inner_in, gate_in, skip_in, gain_in)

    mixed, front_back = jax.vjp(
        mamba_front,
        step_size,
        log_decay,
        inner_vals,
        input_map,
        output_map,
        state_in,
        gate_mamba,
        skip_scale,
        inner_whole,
    )
    mixed_low = mixed.astype(jnp.bfloat16)
    branch_mamba = forward_mul(mixed_low.reshape(-1, inner_width), mamba_whole)
    positions = (ctx_index * block_rows + lax.broadcasted_iota(jnp.int32, (block_rows,), 0)).astype(
        jnp.float32
    )
    query_pre = front_one[:, inner_width:].reshape(seq_count, block_rows, QH, HD)
    key_pre = front_two[:, 1792:2048].reshape(seq_count, block_rows, KVH, HD)
    value_pre = front_two[:, 2048:2304].reshape(seq_count, block_rows, KVH, HD)
    queries = rotate(query_pre, positions, 1.0).astype(jnp.bfloat16)
    keys_rot = rotate(key_pre, positions, 1.0).astype(jnp.bfloat16)
    values = value_pre.astype(jnp.bfloat16)
    ctx_size = lax.axis_size("ctx")
    ctx_order = index_bits("ctx")
    both = grown(jnp.concatenate([keys_rot, values], axis=2), ctx_order)
    both = both.transpose(1, 0, 2, 3, 4).reshape(seq_count, -1, 2 * KVH, HD)
    keys_all, values_all = both[:, :, :KVH], both[:, :, KVH:]
    segment_all = grown(segment_ids.astype(jnp.bfloat16), ctx_order)
    segment_all = segment_all.transpose(1, 0, 2).reshape(seq_count, -1)
    grouped = queries.reshape(seq_count, block_rows, KVH, group_size, HD)
    allowed = attention_mask(positions, segment_ids, segment_all.astype(jnp.float32))
    scores = score_block(grouped, keys_all, allowed)
    row_max = jnp.max(scores, axis=-1, keepdims=True)
    log_total = row_max + jnp.log(jnp.sum(jnp.exp(scores - row_max), axis=-1, keepdims=True))
    attend = jnp.exp(scores - log_total).astype(jnp.bfloat16)
    attended = jnp.einsum(
        "skgij,sjkd->sikgd", attend, values_all, preferred_element_type=jnp.float32
    ).astype(jnp.bfloat16)
    branch_attn = forward_mul(attended.reshape(-1, QH * HD), attn_whole)
    residual = flat_rows + branch_mamba + branch_attn
    feed_scale = feed_whole
    normed_two = gained_norm(residual, feed_scale).astype(jnp.bfloat16)
    feed_gate_out = forward_mul(normed_two, gate_whole)
    feed_up_out = forward_mul(normed_two, up_whole)
    feed_hidden = (jax.nn.silu(feed_gate_out) * feed_up_out).astype(jnp.bfloat16)
    output = (
        (residual + forward_mul(feed_hidden, down_whole))
        .astype(jnp.bfloat16)
        .reshape(seq_count, block_rows, model_width)
    )
    upstream = cotangent.reshape(-1, model_width)
    grad_feed_down = outer_sum(feed_hidden, upstream)
    grad_hidden = back_mul(upstream, down_whole)
    _, swiglu_back = jax.vjp(
        lambda gate_arg, up_arg: jax.nn.silu(gate_arg) * up_arg, feed_gate_out, feed_up_out
    )
    grad_gate_ff, grad_up_ff = swiglu_back(grad_hidden)
    gate_ff_low = grad_gate_ff.astype(jnp.bfloat16)
    up_ff_low = grad_up_ff.astype(jnp.bfloat16)
    grad_feed_gate = outer_sum(normed_two, gate_ff_low)
    grad_feed_up = outer_sum(normed_two, up_ff_low)
    grad_normed_two = back_mul(gate_ff_low, gate_whole) + back_mul(
        up_ff_low, up_whole
    )
    _, norm_two_back = jax.vjp(gained_norm, residual, feed_whole)
    grad_res_norm, grad_feed_gain = norm_two_back(grad_normed_two)
    grad_residual = upstream.astype(jnp.float32) + grad_res_norm
    residual_low = grad_residual.astype(jnp.bfloat16)
    grad_mamba_proj = outer_sum(mixed_low.reshape(-1, inner_width), residual_low)
    grad_attn_proj = outer_sum(attended.reshape(-1, QH * HD), residual_low)
    grad_mixed = back_mul(residual_low, mamba_whole).reshape(
        seq_count, block_rows, inner_width
    )
    grad_attended = (
        back_mul(residual_low, attn_whole)
        .astype(jnp.bfloat16)
        .reshape(seq_count, block_rows, KVH, group_size, HD)
    )
    scores_again = score_block(grouped, keys_all, allowed)
    attend_full = jnp.exp(scores_again - log_total)
    attend_again = attend_full.astype(jnp.bfloat16)
    grad_attend = jnp.einsum(
        "sikgd,sjkd->skgij", grad_attended, values_all, preferred_element_type=jnp.float32
    )
    grad_values_all = jnp.einsum(
        "skgij,sikgd->sjkd", attend_again, grad_attended, preferred_element_type=jnp.float32
    )
    row_dot = jnp.sum(attend_full * grad_attend, axis=-1, keepdims=True)
    grad_scores = (attend_full * (grad_attend - row_dot)).astype(jnp.bfloat16)
    grad_queries = jnp.einsum(
        "skgij,sjkd->sikgd", grad_scores, keys_all, preferred_element_type=jnp.float32
    ) * HD ** (-0.5)
    grad_keys_all = jnp.einsum(
        "skgij,sikgd->sjkd", grad_scores, grouped, preferred_element_type=jnp.float32
    ) * HD ** (-0.5)
    grad_both = jnp.concatenate([grad_keys_all, grad_values_all], axis=2).astype(jnp.bfloat16)
    grad_both = grad_both.reshape(seq_count, ctx_size, block_rows, 2 * KVH, HD)
    grad_both = shrunk(grad_both.transpose(1, 0, 2, 3, 4), ctx_order)
    grad_keys, grad_values = grad_both[:, :, :KVH], grad_both[:, :, KVH:]
    query_low = (
        rotate(grad_queries.reshape(seq_count, block_rows, QH, HD), positions, -1.0)
        .astype(jnp.bfloat16)
        .reshape(-1, QH * HD)
    )
    key_low = rotate(grad_keys, positions, -1.0).astype(jnp.bfloat16).reshape(-1, KVH * HD)
    value_low = grad_values.astype(jnp.bfloat16).reshape(-1, KVH * HD)
    front_grads = front_back(grad_mixed)
    chain_grads = entering((block_decay, front_grads[5]), "ctx", chain_combine, identity_pair)
    grad_state_out = chain_grads[1]
    grad_decay = jnp.sum(grad_state_out * state_in, axis=(2, 3))
    summary_grads = summary_back((grad_decay, grad_state_out))
    (
        grad_extended,
        grad_step_raw,
        grad_conv_taps,
        grad_conv_bias,
        grad_step_bias,
        grad_decay_log,
    ) = prepare_back(
        (
            front_grads[2] + summary_grads[2],
            front_grads[3] + summary_grads[3],
            front_grads[4],
            front_grads[0] + summary_grads[0],
            front_grads[1] + summary_grads[1],
        )
    )
    back_rows = shifted(grad_extended[:, : tap_count - 1].astype(jnp.bfloat16), "ctx", -1).astype(
        jnp.float32
    )
    grad_conv_input = (
        grad_extended[:, tap_count - 1 :].at[:, block_rows - tap_count + 1 :].add(back_rows)
    )
    gate_low = front_grads[6].astype(jnp.bfloat16).reshape(-1, inner_width)
    conv_low = grad_conv_input.astype(jnp.bfloat16).reshape(-1, grad_conv_input.shape[-1])
    step_low = grad_step_raw.astype(jnp.bfloat16).reshape(-1, MH)
    lows_one = jnp.concatenate([gate_low, query_low], axis=1)
    lows_two = jnp.concatenate([conv_low, key_low, value_low], axis=1)
    step_wide = jnp.pad(step_low, ((0, 0), (0, 128 - MH)))
    grad_one = outer_sum(normed, lows_one)
    grad_two = outer_sum(normed, lows_two)
    grad_step = outer_sum(normed, step_low)
    grad_normed = back_mul(lows_one, pack_one) + back_mul(
        jnp.concatenate([lows_two, step_wide], axis=1), pack_two
    )
    _, norm_one_back = jax.vjp(gained_norm, flat_rows, pre_whole)
    grad_flat, grad_pre_gain = norm_one_back(grad_normed)
    grad_tokens = (grad_residual + grad_flat).reshape(seq_count, block_rows, model_width)
    device_count = lax.axis_size("dp") * ctx_size
    small_grads = jnp.concatenate(
        [
            grad_pre_gain.reshape(device_count, -1),
            grad_feed_gain.reshape(device_count, -1),
            front_grads[8].reshape(device_count, -1),
            grad_conv_bias.reshape(device_count, -1),
            grad_conv_taps.reshape(KC, device_count, -1)
            .transpose(1, 0, 2)
            .reshape(device_count, -1),
        ],
        axis=1,
    )
    small_grads = jnp.pad(
        small_grads, ((0, 0), (0, shard_rows * 16 - small_grads.shape[1]))
    ).reshape(-1, 16)
    step_grads = jnp.pad(
        jnp.concatenate([grad_step, small_grads], axis=1), ((0, 0), (0, 128 - MH - 16))
    )
    low = jnp.bfloat16
    gates = (grad_queries, front_grads[5], summary_grads[2])
    own_down = scatter_rows(grad_feed_down.astype(low), down_rows, False, gates)
    own_gate = scatter_rows(grad_feed_gate.astype(low), shard_rows, False, gates)
    own_up = scatter_rows(grad_feed_up.astype(low), shard_rows, True, gates)
    own_mix = scatter_rows(
        jnp.concatenate(
            [
                grad_mamba_proj.astype(low).reshape(device_count, inner_rows, -1),
                grad_attn_proj.astype(low).reshape(device_count, attn_rows, -1),
            ],
            axis=1,
        ).reshape(device_count * (inner_rows + attn_rows), -1),
        inner_rows + attn_rows,
        True,
        gates,
    )
    own_one = scatter_rows(grad_one.astype(low), shard_rows, False)
    own_two = scatter_rows(
        jnp.concatenate([grad_two.astype(low), step_grads.astype(low)], axis=1), shard_rows, True
    )
    own_small = own_two[:, 2304 + MH : 2304 + MH + 16].reshape(-1)
    head_sums = butterfly_sum(jnp.stack([grad_decay_log, grad_step_bias, front_grads[7]]))
    return (
        output,
        grad_tokens,
        own_small[cuts[0] : cuts[1]],
        own_one[:, :inner_width],
        own_two[:, :1792],
        own_two[:, 2304 : 2304 + MH],
        own_small[cuts[4] : cuts[5]].reshape(KC, feat_rows),
        own_small[cuts[3] : cuts[4]],
        head_sums[0],
        head_sums[1],
        head_sums[2],
        own_small[cuts[2] : cuts[3]],
        own_mix[:inner_rows],
        own_one[:, inner_width:],
        own_two[:, 1792:2048],
        own_two[:, 2048:2304],
        own_mix[inner_rows:],
        own_small[cuts[1] : cuts[2]],
        own_gate,
        own_up,
        own_down,
    )


def solution(mesh):
    return jax.shard_map(
        body,
        mesh=mesh,
        in_specs=(
            P("dp", "ctx", None),
            P("dp", "ctx"),
            P(("dp", "ctx")),
            P(("dp", "ctx"), None),
            P(("dp", "ctx"), None),
            P(("dp", "ctx"), None),
            P(None, ("dp", "ctx")),
            P(("dp", "ctx")),
            P(),
            P(),
            P(),
            P(("dp", "ctx")),
            P(("dp", "ctx"), None),
            P(("dp", "ctx"), None),
            P(("dp", "ctx"), None),
            P(("dp", "ctx"), None),
            P(("dp", "ctx"), None),
            P(("dp", "ctx")),
            P(("dp", "ctx"), None),
            P(("dp", "ctx"), None),
            P(("dp", "ctx"), None),
            P("dp", "ctx", None),
        ),
        out_specs=(
            P("dp", "ctx", None),
            P("dp", "ctx", None),
            P(("dp", "ctx")),
            P(("dp", "ctx"), None),
            P(("dp", "ctx"), None),
            P(("dp", "ctx"), None),
            P(None, ("dp", "ctx")),
            P(("dp", "ctx")),
            P(),
            P(),
            P(),
            P(("dp", "ctx")),
            P(("dp", "ctx"), None),
            P(("dp", "ctx"), None),
            P(("dp", "ctx"), None),
            P(("dp", "ctx"), None),
            P(("dp", "ctx"), None),
            P(("dp", "ctx")),
            P(("dp", "ctx"), None),
            P(("dp", "ctx"), None),
            P(("dp", "ctx"), None),
        ),
        check_vma=False,
    )
```
